512 devices in a mesh: prow: 32 (over x, y, core), pcol: 16 (over z).
Axes of the slice: x: 4, y: 4, z: 16, core: 2. Of those that a mesh axis runs over, the one named last changes fastest.
Arguments:
- matrix: float32 [16384, 8192], P('prow', 'pcol'), may hold values from -6 to 6
- pivots: int32 [4, 256], replicated, may hold values from 256 to 16383, as said below
- block_inverses: bfloat16 [4, 256, 256], replicated, may hold values from -1 to 1, as said below
Outputs:
- factored: float32 [16384, 8192], P('prow', 'pcol')
The draws below stay inside these ranges and needn't reach their ends.
Inputs may be any that keep to these rules, and one draw needn't show every extreme that they name: Within step k the 256 pivots pivots[k, j] are distinct rows at or after (k + 1) * 256. Taking together the rows of all row blocks b with the same b mod 32, each such set holds at most 16 of one step's pivots, and in every step one set holds exactly 16. `block_inverses`: the diagonal of every block is positive.
All inputs are finite; a program needn't handle non-finite values.
Results may differ from the reference program's by a relative error of at most 0.0003.
Values sent between devices are 32-bit elements; how exact they have to be, the bound alone decides.
A program may use at most 64 MiB of HBM per device.

```python
import jax
import jax.numpy as jnp
from jax import lax

NB = 256
KSTEPS = 4
RB = 2
CB = 2
GRID_ROWS = 32
GRID_COLS = 16
ROWS = 16384
COLS = 8192
CAP = 16


def draw_pivots(key, part):
    key = jax.random.fold_in(key, 11)
    local_rows = RB * NB
    result = []
    for panel_step in range(KSTEPS):
        step_key = jax.random.fold_in(key, panel_step)
        sub_keys = jax.random.split(step_key, 4)
        favored = jax.random.randint(sub_keys[0], (), 0, GRID_ROWS)
        slot_order = jax.random.permutation(sub_keys[1], GRID_ROWS * CAP)
        not_favored = (slot_order // CAP != favored).astype(jnp.int32)
        picked = slot_order[jnp.argsort(not_favored, stable=True)][:NB]
        picked = jax.random.permutation(sub_keys[2], picked)
        owners = picked // CAP
        slot_ranks = picked % CAP
        scores = jax.vmap(lambda sub_key: jax.random.permutation(sub_key, local_rows))(jax.random.split(sub_keys[3], GRID_ROWS))
        blocks = jnp.arange(local_rows)[None, :] // NB * GRID_ROWS + jnp.arange(GRID_ROWS)[:, None]
        scores = scores.astype(jnp.int32) + local_rows * (blocks > panel_step).astype(jnp.int32)
        chosen = lax.top_k(scores, CAP)[1]
        local_pick = chosen[owners, slot_ranks]
        result.append((local_pick // NB * GRID_ROWS + owners) * NB + local_pick % NB)
    return jnp.stack(result).astype(jnp.int32)


def draw_block_inverses(key, part):
    key = jax.random.fold_in(key, 23)
    sub_keys = jax.random.split(key, 2)
    inv_scale = NB ** (-0.5)
    spread_draw = jnp.clip(jax.random.normal(sub_keys[0], (KSTEPS, NB, NB)), -4.0, 4.0)
    diagonal = jax.random.uniform(sub_keys[1], (KSTEPS, NB), minval=0.25, maxval=0.5)
    row_index = jnp.arange(NB)[:, None]
    col_index = jnp.arange(NB)[None, :]
    values = jnp.where(row_index > col_index, 0.5 * inv_scale * spread_draw, 0.25 * inv_scale * inv_scale * spread_draw)
    values = jnp.where(row_index == col_index, inv_scale * diagonal[:, :, None], values)
    return values.astype(jnp.bfloat16)


def level_of(rng, shape, shards, low, largest):
    loudness, own = 1.0, jax.random.fold_in(rng, 6)
    for position, shards_of in shards:
        draws = jnp.exp(jax.random.uniform(jax.random.fold_in(own, position), (shards_of,), jnp.float32, low / len(shards), largest / len(shards)))
        loudness = loudness * jnp.repeat(draws, shape[position] // shards_of).reshape([-1 if axis == position else 1 for axis in range(len(shape))])
    return loudness


def gaussian(rng, shape, scale, reach, pieces=(), held_as=jnp.bfloat16):
    array = jax.random.normal(rng, shape, jnp.float32) * scale
    if len(pieces) > 0:
        array = level_of(rng, shape, pieces, -0.22, 0.18) * array
    return jnp.clip(array, min=-reach, max=reach).astype(held_as)


def setup_inputs(seed: int = 0) -> dict:
    key_list = jax.random.split(jax.random.key(seed), 4)
    matrix = gaussian(key_list[0], (ROWS, COLS), 1.0, 6.0, ((0, 32), (1, 16)), jnp.float32)
    pivots = draw_pivots(jax.random.fold_in(key_list[3], 71), 0)
    block_inverses = draw_block_inverses(jax.random.fold_in(key_list[3], 71), 0)
    return dict(matrix=matrix, pivots=pivots, block_inverses=block_inverses)


def exact_dot(left, right):
    return jnp.dot(left, right, precision=lax.Precision.HIGHEST, preferred_element_type=jnp.float32)


def reorder(stored_matrix, first_rows, second_rows, first_cols, second_cols):
    shaped = stored_matrix.reshape(first_rows, second_rows, NB, first_cols, second_cols, NB)
    return shaped.transpose(1, 0, 2, 4, 3, 5).reshape(ROWS, COLS)


def reference(matrix, pivots, block_inverses):
    global_matrix = reorder(matrix, GRID_ROWS, RB, GRID_COLS, CB)
    identity = jnp.eye(NB, dtype=jnp.float32)
    for panel_step in range(KSTEPS):
        def swap_rows(index, row_order):
            first = jnp.int32(panel_step * NB) + index.astype(jnp.int32)
            second = pivots[panel_step, index].astype(jnp.int32)
            first_value = row_order[first]
            second_value = row_order[second]
            return row_order.at[first].set(second_value).at[second].set(first_value)

        row_order = lax.fori_loop(0, NB, swap_rows, jnp.arange(ROWS, dtype=jnp.int32))
        global_matrix = jnp.take(global_matrix, row_order, axis=0)
        inverse = block_inverses[panel_step].astype(jnp.float32)
        upper_inverse = jnp.triu(inverse)
        lower_inverse = jnp.tril(inverse, -1) + identity
        top = panel_step * NB
        below = top + NB
        panel_factor = exact_dot(global_matrix[below:, top:below], upper_inverse)
        top_factor = exact_dot(lower_inverse, global_matrix[top:below, below:])
        trailing = global_matrix[below:, below:] - exact_dot(panel_factor, top_factor)
        top_rows = jnp.concatenate([global_matrix[top:below, :below], top_factor], axis=1)
        low_rows = jnp.concatenate([global_matrix[below:, :top], panel_factor, trailing], axis=1)
        global_matrix = jnp.concatenate([global_matrix[:top], top_rows, low_rows], axis=0)
    return reorder(global_matrix, RB, GRID_ROWS, CB, GRID_COLS)
```

```python
import jax
import jax.numpy as jnp
from jax import lax
from jax.experimental import pallas as pl
from jax.experimental.pallas import tpu as pltpu
from jax.sharding import PartitionSpec as P

NB = 256
STEPS = 4
CAP = 16
SLOTS = STEPS * CAP
TOPS = 32
PIECE = SLOTS + TOPS
SIDE = 4
PROWS = 32
RING = 16
WIDE = 512
PAN = STEPS * NB
F32 = jnp.float32
MIB = 1024 * 1024


def prep_kernel(coord, piv_ref, a_ref, packed_ref, source_ref, slot_row_ref, slot_source_ref):
    me = coord[0].astype(F32)
    sub = lax.broadcasted_iota(jnp.int32, (NB, NB), 0)
    lane = lax.broadcasted_iota(jnp.int32, (NB, NB), 1)
    lane_row = lax.broadcasted_iota(jnp.int32, (1, NB), 1).astype(F32)
    lane_slot = lax.broadcasted_iota(jnp.int32, (NB, 128), 1).astype(F32)
    sub_slot = lax.broadcasted_iota(jnp.int32, (CAP, NB), 0).astype(F32)
    lane_wide = lax.broadcasted_iota(jnp.int32, (CAP, WIDE), 1).astype(F32)

    def column(row):
        return jnp.sum(jnp.where(sub == lane, row, 0.0), axis=1, keepdims=True)

    def pick(mask, value):
        return jnp.sum(jnp.where(mask, value, 0.0), axis=0, keepdims=True)

    def top_index(row):
        t = row.astype(jnp.int32)
        return ((t & 255) >> 3) * PIECE + SLOTS + (t >> 8) * 8 + (t & 7)

    source_ref[...] = jnp.zeros_like(source_ref)
    slot_row_ref[...] = jnp.zeros_like(slot_row_ref)
    slot_source_ref[...] = jnp.zeros_like(slot_source_ref)
    pivot_cols, moved_cols = [], []
    for k in range(STEPS):
        pivot = piv_ref[k : k + 1, :]
        owner = ((pivot >> 8) & 31).astype(F32)
        local = (((pivot >> 13) << 8) | (pivot & 255)).astype(F32)
        pivot = pivot.astype(F32)
        owner_col, local_col, pivot_col = column(owner), column(local), column(pivot)
        rank = pick((owner_col == owner) & (sub < lane), 1.0)
        rank_col = column(rank)
        position = lane_row + float(k * NB)
        moved = position
        source = (owner * PIECE + float(k * CAP) + rank).astype(jnp.int32)
        for earlier in range(k):
            same = pivot_cols[earlier] == position
            moved = jnp.where(pick(same, 1.0) > 0.0, pick(same, moved_cols[earlier]), moved)
            same = pivot_cols[earlier] == pivot
            source = jnp.where(
                pick(same, 1.0) > 0.0, top_index(pick(same, moved_cols[earlier])), source
            )
        moved_col = column(moved)
        pivot_cols.append(pivot_col)
        moved_cols.append(moved_col)
        source_ref[k : k + 1, :] = source
        mine = (owner_col == me) & (rank_col == lane_slot)
        filled = pick(mine, 1.0) > 0.0
        slot_row_ref[k : k + 1, :] = jnp.where(filled, pick(mine, local_col), float(WIDE)).astype(
            jnp.int32
        )
        slot_source_ref[k : k + 1, :] = top_index(jnp.where(filled, pick(mine, moved_col), 0.0))
        mine = (owner == me) & (rank == sub_slot)
        row = jnp.sum(jnp.where(mine, local, 0.0), axis=1, keepdims=True)
        packed_ref[k * CAP : (k + 1) * CAP, :] = jnp.dot(
            jnp.where(row == lane_wide, 1.0, 0.0),
            a_ref[...],
            precision=lax.Precision.HIGHEST,
            preferred_element_type=F32,
        )


def remote(src, dst, send_sem, recv_sem, target):
    return pltpu.make_async_remote_copy(
        src_ref=src,
        dst_ref=dst,
        send_sem=send_sem,
        recv_sem=recv_sem,
        device_id=target,
        device_id_type=pl.DeviceIdType.MESH,
    )


def place(x, y, core):
    return (lax.rem(x, SIDE) * SIDE + lax.rem(y, SIDE)) * 2 + core


GATHER_SEMS = 72


def plane_gather(view, rows, send_sem, recv_sem, sent):
    me = lax.axis_index("prow")
    core = lax.rem(me, 2)
    chip = me // 2
    cx, cy = chip // SIDE, lax.rem(chip, SIDE)
    half, part = rows // 2, rows // 4

    def at(h, i, j, c):
        return place(cx + i, cy + j, c) if h == 0 else place(cx + j, cy + i, c)

    def start(index, target, piece, row, count):
        copy = remote(
            view(piece, row, count),
            view(piece, row, count),
            send_sem.at[index],
            recv_sem.at[index],
            {"prow": target},
        )
        copy.start()
        sent.append(copy)

    def arrive(index, piece, row, count):
        remote(
            view(piece, row, count),
            view(piece, row, count),
            send_sem.at[index],
            recv_sem.at[index],
            {"prow": me},
        ).wait_recv()

    def first(h, n):
        return h * 4 + n

    def second(h, i, n):
        return 8 + (h * 4 + i) * 4 + n

    def across(h, i, j):
        return 40 + (h * 4 + i) * 4 + j

    def to_core(h, i, j):
        start(across(h, i, j), place(cx, cy, 1 - core), at(h, i, j, core), h * half, half)

    def start_second(h, i):
        piece = at(h, i, 0, core)
        start(second(h, i, 0), at(h, 0, 1, core), piece, h * half, half)
        start(second(h, i, 1), at(h, 0, 3, core), piece, h * half, half)

    for h in (0, 1):
        start(first(h, 0), at(h, 1, 0, core), me, h * half, half)
        start(first(h, 1), at(h, 3, 0, core), me, h * half, half)
    for h in (0, 1):
        start_second(h, 0)
        to_core(h, 0, 0)
    yield
    for n, i, on in ((0, 3, 1), (1, 1, 3)):
        for h in (0, 1):
            piece = at(h, i, 0, core)
            arrive(first(h, n), piece, h * half, half)
            start(first(h, 2 + n), at(h, on, 0, core), piece, h * half + n * part, part)
            start_second(h, i)
            to_core(h, i, 0)
            yield
    for h in (0, 1):
        for n in (0, 1):
            arrive(first(h, 2 + n), at(h, 2, 0, core), h * half + n * part, part)
        start_second(h, 2)
        to_core(h, 2, 0)
        yield
    for i in (0, 3, 1, 2):
        for n, j, on in ((0, 3, 1), (1, 1, 3)):
            for h in (0, 1):
                piece = at(h, i, j, core)
                arrive(second(h, i, n), piece, h * half, half)
                start(second(h, i, 2 + n), at(h, 0, on, core), piece, h * half + n * part, part)
                to_core(h, i, j)
                yield
    for i in (0, 3, 1, 2):
        for h in (0, 1):
            for n in (0, 1):
                arrive(second(h, i, 2 + n), at(h, i, 2, core), h * half + n * part, part)
            to_core(h, i, 2)
            yield
    for j in (0, 3, 1, 2):
        for i in (0, 3, 1, 2):
            for h in (0, 1):
                arrive(across(h, i, j), at(h, i, j, 1 - core), h * half, half)


class RingSpread:
    def __init__(self, view, per_source, send_sem, recv_sem):
        self.view, self.count = view, per_source
        self.send_sem, self.recv_sem = send_sem, recv_sem
        z = lax.axis_index("pcol")
        self.z = z
        self.lows = [self.range_in(0, z), self.range_in(1, z)]
        up = self.range_in(0, z + 1)
        down_low, down_high = self.range_in(1, lax.rem(z + RING - 1, RING))
        last = z == RING - 1
        self.outs = [
            (jnp.where(last, 0, up[0]), jnp.where(last, 0, up[1])),
            (down_low, down_high),
        ]
        self.to = [{"pcol": lax.rem(z + 1, RING)}, {"pcol": lax.rem(z + RING - 1, RING)}]
        inner = z < STEPS
        self.lag = [
            jnp.where(inner, 3, (z - 3) * 5 // 2),
            jnp.where(inner, 3, (RING - z) * 5 // 2),
        ]
        self.steps = max(3 * per_source + 3, 2 * per_source + 20)

    def meet(self, z):
        c = self.count
        return jnp.clip(2 * c + ((19 - 2 * z) * 5) // 4, 0, 4 * c)

    def range_in(self, way, z):
        c = self.count
        far = z >= STEPS
        if way == 0:
            return jnp.where(far, 0, (4 - z) * c), jnp.where(far, self.meet(z), 4 * c)
        return jnp.where(far, self.meet(z), 0), jnp.where(far, 4 * c, (3 - z) * c)

    def copy(self, way, g):
        return remote(
            self.view(g),
            self.view(g),
            self.send_sem.at[way, g],
            self.recv_sem.at[way, g],
            self.to[way],
        )

    def pass_on(self, way, g):
        low, high = self.outs[way]

        @pl.when((g >= low) & (g < high))
        def _():
            self.copy(way, g).start()

    def start(self):
        c = self.count

        @pl.when(self.z < STEPS)
        def _():
            @pl.loop(0, c)
            def _(i):
                self.pass_on(0, (3 - self.z) * c + i)
                self.pass_on(1, (4 - self.z) * c - 1 - i)

    def run(self, begin, end):
        if end <= begin:
            return

        @pl.loop(begin, end)
        def _(t):
            for way in (0, 1):
                low, high = self.lows[way]
                i = t - self.lag[way]

                @pl.when((i >= 0) & (i < high - low))
                def _():
                    g = low + i if way == 0 else high - 1 - i
                    self.copy(way, g).wait_recv()
                    self.pass_on(way, g)

    def finish(self):
        for way in (0, 1):
            low, high = self.outs[way]

            @pl.loop(low, high)
            def _(g):
                self.copy(way, g).wait_send()


def neighbours():
    me, z = lax.axis_index("prow"), lax.axis_index("pcol")
    core, chip = lax.rem(me, 2), me // 2
    cx, cy = chip // SIDE, lax.rem(chip, SIDE)
    return [
        {"prow": place(cx + 1, cy, core)},
        {"prow": place(cx + 3, cy, core)},
        {"prow": place(cx, cy + 1, core)},
        {"prow": place(cx, cy + 3, core)},
        {"prow": place(cx, cy, 1 - core)},
        {"pcol": lax.rem(z + 1, RING)},
        {"pcol": lax.rem(z + RING - 1, RING)},
    ]


def greet(targets):
    barrier = pltpu.get_barrier_semaphore()
    for target in targets:
        pl.semaphore_signal(
            barrier, inc=1, device_id=target, device_id_type=pl.DeviceIdType.MESH
        )
    return barrier


CHUNK = 32


def raw_kernel(
    source_ref, slot_source_ref, a_ref, packed_ref,
    cand_ref, panels_ref, piece_ref, moved_ref,
    slot_send, slot_recv, top_send, top_recv, deal_send, deal_recv, ring_send, ring_recv,
):
    me, z = lax.axis_index("prow"), lax.axis_index("pcol")
    barrier = greet(neighbours())
    for p in range(STEPS):

        @pl.when(me != p)
        def _():
            pl.semaphore_signal(
                barrier, inc=1, device_id={"prow": p}, device_id_type=pl.DeviceIdType.MESH
            )

    own = pl.multiple_of(me * PIECE, 8)
    cand_ref[pl.ds(own, SLOTS), :] = packed_ref[...]
    for p in range(STEPS):

        @pl.when(me == p)
        def _():
            cand_ref[pl.ds(own + SLOTS + 8 * p, 8), :] = a_ref[8 * p : 8 * p + 8, :]

        @pl.when(z == p)
        def _():
            panels_ref[p] = a_ref[:, 0:NB]

    pl.semaphore_wait(barrier, jnp.where(me < STEPS, 7 + PROWS - 1, 7))

    def deal(p, target):
        rows = pl.ds(pl.multiple_of(target * PIECE + SLOTS + 8 * p, 8), 8)
        return remote(
            a_ref.at[pl.ds(pl.multiple_of(target * 8, 8), 8), :],
            cand_ref.at[rows, :],
            deal_send.at[target],
            deal_recv.at[p],
            {"prow": target},
        )

    @pl.when(me < STEPS)
    def _():
        @pl.loop(1, PROWS)
        def _(i):
            deal(me, lax.rem(me + i, PROWS)).start()

    def chunk(g):
        per = WIDE // CHUNK
        return panels_ref.at[
            3 - g // per, pl.ds(pl.multiple_of(lax.rem(g, per) * CHUNK, CHUNK), CHUNK), :
        ]

    ring = RingSpread(chunk, WIDE // CHUNK, ring_send, ring_recv)

    def slot_view(piece, row, count):
        return cand_ref.at[pl.ds(pl.multiple_of(piece * PIECE + row, 8), count), :]

    def top_view(piece, row, count):
        return cand_ref.at[pl.ds(pl.multiple_of(piece * PIECE + SLOTS + row, 8), count), :]

    sent = []
    ring.start()
    done = 0
    for _ in plane_gather(slot_view, SLOTS, slot_send, slot_recv, sent):
        ring.run(done, done + 1)
        done += 1
    for p in range(STEPS):

        @pl.when(me != p)
        def _():
            deal(p, me).wait_recv()

    for n, _ in enumerate(plane_gather(top_view, TOPS, top_send, top_recv, sent)):
        if n % 2 == 0:
            ring.run(done, done + 1)
            done += 1

    def row_of(index):
        return cand_ref[pl.ds(index, 1), :]

    @pl.loop(0, 32)
    def _(i):
        piece_ref[pl.ds(i, 1), :] = row_of(
            source_ref[me // 8, lax.rem(me, 8) * 32 + i]
        )[:, 0:NB]

    @pl.loop(0, CAP)
    def _(i):
        for k in range(STEPS):
            moved_ref[pl.ds(k * CAP + i, 1), :] = row_of(slot_source_ref[k, i])

    ring.run(done, ring.steps)
    for copy in sent:
        copy.wait_send()
    ring.finish()

    @pl.when(me < STEPS)
    def _():
        @pl.loop(1, PROWS)
        def _(i):
            deal(me, lax.rem(me + i, PROWS)).wait_send()


def top_kernel(
    piece_ref, moved_ref, corner_ref, moved_panels_ref,
    plane_send, plane_recv, first_send, first_recv, ring_send, ring_recv,
):
    me, z = lax.axis_index("prow"), lax.axis_index("pcol")
    barrier = greet(neighbours())
    own = pl.multiple_of(me * 128, 128)
    for p in range(STEPS):

        @pl.when(z == p)
        def _():
            corner_ref[pl.ds(own + 32 * p, 32), :] = piece_ref[...]
            moved_panels_ref[p] = moved_ref[:, 0:NB]

    pl.semaphore_wait(barrier, 7)

    def first_view(g):
        return corner_ref.at[pl.ds(pl.multiple_of(own + (3 - g) * 32, 32), 32), :]

    def moved_view(g):
        per = SLOTS // CHUNK
        return moved_panels_ref.at[
            3 - g // per, pl.ds(pl.multiple_of(lax.rem(g, per) * CHUNK, CHUNK), CHUNK), :
        ]

    def corner_view(piece, row, count):
        return corner_ref.at[pl.ds(pl.multiple_of(piece * 128 + row, 32), count), :]

    first = RingSpread(first_view, 1, first_send, first_recv)
    ring = RingSpread(moved_view, SLOTS // CHUNK, ring_send, ring_recv)
    first.start()
    first.run(0, 45)
    ring.start()
    sent = []
    done = 0
    for _ in plane_gather(corner_view, 128, plane_send, plane_recv, sent):
        ring.run(done, done + 1)
        done += 1
    ring.run(done, 45)
    for copy in sent:
        copy.wait_send()
    first.finish()
    ring.finish()


def split(value):
    high = value.astype(jnp.bfloat16)
    return high, (value - high.astype(F32)).astype(jnp.bfloat16)


def dot(left, right):
    return jnp.dot(left, right, preferred_element_type=F32)


def eliminate_kernel(
    coord, source_ref, slot_row_ref, slot_source_ref, a_ref, cand_ref, panels_ref,
    corner_ref, moved_panels_ref, inv_ref, out_ref, work, high_ref, low_ref, keep,
):
    me, z = coord[0], coord[1]
    here = PAN
    for piece in range(PROWS):
        for q in range(STEPS):
            work[piece * 32 : piece * 32 + 32, q * NB : (q + 1) * NB] = corner_ref[
                piece * 128 + q * 32 : piece * 128 + q * 32 + 32, :
            ]
    for q in range(STEPS):
        work[here : here + WIDE, q * NB : (q + 1) * NB] = panels_ref[q]
    work[here : here + WIDE, PAN:] = a_ref[...]
    for k in range(STEPS):

        @pl.loop(0, NB, unroll=8)
        def _(j):
            work[pl.ds(k * NB + j, 1), PAN:] = cand_ref[pl.ds(source_ref[k, j], 1), :]

    for k in range(STEPS):

        @pl.loop(0, CAP)
        def _(s):
            row = pl.ds(here + slot_row_ref[k, s], 1)
            work[row, PAN:] = cand_ref[pl.ds(slot_source_ref[k, s], 1), :]
            for q in range(STEPS):
                work[row, q * NB : (q + 1) * NB] = moved_panels_ref[
                    q, pl.ds(k * CAP + s, 1), :
                ]

    row_i = lax.broadcasted_iota(jnp.int32, (NB, NB), 0)
    col_i = lax.broadcasted_iota(jnp.int32, (NB, NB), 1)
    total = PAN + WIDE
    for k in range(STEPS):
        top, begin = k * NB, (k + 1) * NB
        inverse = inv_ref[k].astype(F32)
        upper = jnp.where(row_i <= col_i, inverse, 0.0).astype(jnp.bfloat16)
        lower = jnp.where(
            row_i > col_i, inverse, jnp.where(row_i == col_i, 1.0, 0.0)
        ).astype(jnp.bfloat16)

        @pl.when(me == k)
        def _():
            keep[...] = work[top : top + NB, PAN : PAN + NB]

        for c in range(begin, total, NB):
            high, low = split(work[top : top + NB, c : c + NB])
            solved = dot(lower, high) + dot(lower, low)
            work[top : top + NB, c : c + NB] = solved
            high_ref[:, c : c + NB], low_ref[:, c : c + NB] = split(solved)

        @pl.loop(begin // NB, total // NB)
        def _(r):
            rows = pl.ds(pl.multiple_of(r * NB, NB), NB)
            high, low = split(work[rows, top : top + NB])
            factor = dot(high, upper) + dot(low, upper)
            work[rows, top : top + NB] = factor
            high, low = split(factor)
            for c in range(begin, total, NB):
                work[rows, c : c + NB] -= (
                    dot(high, high_ref[:, c : c + NB])
                    + dot(high, low_ref[:, c : c + NB])
                    + dot(low, high_ref[:, c : c + NB])
                )

    out_ref[...] = work[here : here + WIDE, PAN:]
    for q in range(STEPS):

        @pl.when(z == q)
        def _():
            out_ref[:, 0:NB] = work[here : here + WIDE, q * NB : (q + 1) * NB]

    for p in range(STEPS):

        @pl.when(me == p)
        def _():
            out_ref[0:NB, :] = work[p * NB : (p + 1) * NB, PAN:]
            for q in range(p):

                @pl.when(z == q)
                def _():
                    out_ref[0:NB, 0:NB] = work[p * NB : (p + 1) * NB, q * NB : (q + 1) * NB]

            @pl.when(z == p)
            def _():
                out_ref[0:NB, 0:NB] = keep[...]


VMEM = pl.BlockSpec(memory_space=pltpu.VMEM)
SMEM = pl.BlockSpec(memory_space=pltpu.SMEM)


def shape(*dims, dtype=F32):
    return jax.ShapeDtypeStruct(dims, dtype)


def prepare(coord, pivots, matrix):
    return pl.pallas_call(
        prep_kernel,
        out_shape=[
            shape(SLOTS, WIDE),
            shape(8, NB, dtype=jnp.int32),
            shape(8, 128, dtype=jnp.int32),
            shape(8, 128, dtype=jnp.int32),
        ],
        in_specs=[SMEM, VMEM, VMEM],
        out_specs=[VMEM] * 4,
        compiler_params=pltpu.CompilerParams(vmem_limit_bytes=16 * MIB),
    )(coord, pivots, matrix)


def gather_raw(source, slot_source, matrix, packed):
    chunks = STEPS * WIDE // CHUNK
    dma = pltpu.SemaphoreType.DMA
    return pl.pallas_call(
        raw_kernel,
        out_shape=[
            shape(PROWS * PIECE, WIDE),
            shape(STEPS, WIDE, NB),
            shape(32, NB),
            shape(SLOTS, WIDE),
        ],
        in_specs=[SMEM, SMEM, VMEM, VMEM],
        out_specs=[VMEM] * 4,
        scratch_shapes=[
            dma((GATHER_SEMS,)), dma((GATHER_SEMS,)),
            dma((GATHER_SEMS,)), dma((GATHER_SEMS,)),
            dma((PROWS,)), dma((STEPS,)),
            dma((2, chunks)), dma((2, chunks)),
        ],
        compiler_params=pltpu.CompilerParams(
            vmem_limit_bytes=32 * MIB, collective_id=0, has_side_effects=True
        ),
    )(source, slot_source, matrix, packed)


def gather_top(piece, moved):
    chunks = STEPS * SLOTS // CHUNK
    dma = pltpu.SemaphoreType.DMA
    return pl.pallas_call(
        top_kernel,
        out_shape=[shape(PROWS * 128, NB), shape(STEPS, SLOTS, NB)],
        in_specs=[VMEM] * 2,
        out_specs=[VMEM] * 2,
        scratch_shapes=[
            dma((GATHER_SEMS,)), dma((GATHER_SEMS,)),
            dma((2, STEPS)), dma((2, STEPS)),
            dma((2, chunks)), dma((2, chunks)),
        ],
        compiler_params=pltpu.CompilerParams(
            vmem_limit_bytes=32 * MIB, collective_id=1, has_side_effects=True
        ),
    )(piece, moved)


def eliminate(coord, source, slot_row, slot_source, matrix, cand, panels, corner, moved, inverses):
    return pl.pallas_call(
        eliminate_kernel,
        out_shape=shape(WIDE, WIDE),
        in_specs=[SMEM] * 4 + [VMEM] * 6,
        out_specs=VMEM,
        scratch_shapes=[
            pltpu.VMEM((PAN + WIDE + 8, PAN + WIDE), F32),
            pltpu.VMEM((NB, PAN + WIDE), jnp.bfloat16),
            pltpu.VMEM((NB, PAN + WIDE), jnp.bfloat16),
            pltpu.VMEM((NB, NB), F32),
        ],
        compiler_params=pltpu.CompilerParams(vmem_limit_bytes=48 * MIB),
    )(coord, source, slot_row, slot_source, matrix, cand, panels, corner, moved, inverses)


def per_device(matrix, pivots, block_inverses):
    coord = jnp.stack([lax.axis_index("prow"), lax.axis_index("pcol")]).astype(jnp.int32)
    packed, source, slot_row, slot_source = prepare(coord, pivots, matrix)
    cand, panels, piece, moved = gather_raw(source, slot_source, matrix, packed)
    corner, moved_panels = gather_top(piece, moved)
    return eliminate(
        coord, source, slot_row, slot_source, matrix, cand, panels, corner, moved_panels,
        block_inverses,
    )


def solution(mesh):
    placed = (P("prow", "pcol"), P(), P())
    return jax.shard_map(
        per_device, mesh=mesh, in_specs=placed, out_specs=P("prow", "pcol"), check_vma=False
    )
```

```python
import jax
import jax.numpy as jnp
from jax import lax
from jax.experimental import pallas as pl
from jax.experimental.pallas import tpu as pltpu
from jax.sharding import PartitionSpec as P

NB = 256
STEPS = 4
CAP = 16
SLOTS = STEPS * CAP
TOPS = 32
PIECE = SLOTS + TOPS
DEAL = 32
WINDOW = 3
SIDE = 4
PROWS = 32
RING = 16
WIDE = 512
PAN = STEPS * NB
CHUNK = 32
LATE = 32
F32 = jnp.float32
BF16 = jnp.bfloat16
MIB = 1024 * 1024


def prep_kernel(coord, piv_ref, source_ref, slot_ref, local_ref, lanes_ref):
    me = coord[0].astype(F32)
    sub = lax.broadcasted_iota(jnp.int32, (NB, NB), 0)
    lane = lax.broadcasted_iota(jnp.int32, (NB, NB), 1)
    lane_row = lax.broadcasted_iota(jnp.int32, (1, NB), 1).astype(F32)
    lane_slot = lax.broadcasted_iota(jnp.int32, (NB, 128), 1).astype(F32)

    def column(row):
        return jnp.sum(jnp.where(sub == lane, row, 0.0), axis=1, keepdims=True)

    def pick(mask, value):
        return jnp.sum(jnp.where(mask, value, 0.0), axis=0, keepdims=True)

    def top_index(row):
        t = row.astype(jnp.int32)
        return piece_index((t & 255) >> 3) + SLOTS + (t >> 8) * 8 + (t & 7)

    def piece_index(p):
        return ((p & 1) * 16 + (p >> 1)) << 7

    source_ref[...] = jnp.zeros_like(source_ref)
    slot_ref[...] = jnp.zeros_like(slot_ref)
    filled = jnp.zeros((1, 128), F32)
    slot_row = jnp.zeros((1, 128), F32)
    slot_top = jnp.zeros((1, 128), F32)
    pivot_cols, moved_cols = [], []
    for k in range(STEPS):
        pivot = piv_ref[k : k + 1, :]
        owner = ((pivot >> 8) & 31).astype(F32)
        local = (((pivot >> 13) << 8) | (pivot & 255)).astype(F32)
        pivot = pivot.astype(F32)
        owner_col, local_col, pivot_col = column(owner), column(local), column(pivot)
        rank = pick((owner_col == owner) & (sub < lane), 1.0) + float(k * CAP)
        rank_col = column(rank)
        position = lane_row + float(k * NB)
        moved = position
        source = piece_index(owner.astype(jnp.int32)) + rank.astype(jnp.int32)
        mine = jnp.where(owner == me, local, -1.0)
        for earlier in range(k):
            same = pivot_cols[earlier] == position
            moved = jnp.where(pick(same, 1.0) > 0.0, pick(same, moved_cols[earlier]), moved)
            same = pivot_cols[earlier] == pivot
            hit = pick(same, 1.0) > 0.0
            top = pick(same, moved_cols[earlier])
            source = jnp.where(hit, top_index(top), source)
            block = (top.astype(jnp.int32) >> 8).astype(F32)
            mine = jnp.where(hit, jnp.where(block == me, top - block * NB, -1.0), mine)
        moved_col = column(moved)
        pivot_cols.append(pivot_col)
        moved_cols.append(moved_col)
        source_ref[k : k + 1, :] = source
        local_ref[k * NB : (k + 1) * NB, :] = column(mine)
        here = (owner_col == me) & (rank_col == lane_slot)
        filled += pick(here, 1.0)
        slot_row += pick(here, local_col)
        slot_top += pick(here, moved_col)
    slot_ref[0:1, :] = slot_row.astype(jnp.int32)
    slot_ref[1:2, :] = top_index(slot_top) - SLOTS
    lanes_ref[...] = jnp.broadcast_to(jnp.where(filled > 0.0, slot_row, -1.0), (8, 128))


def remote(src, dst, send_sem, recv_sem, target):
    return pltpu.make_async_remote_copy(
        src_ref=src,
        dst_ref=dst,
        send_sem=send_sem,
        recv_sem=recv_sem,
        device_id=target,
        device_id_type=pl.DeviceIdType.MESH,
    )


def place(x, y, core):
    return (lax.rem(x, SIDE) * SIDE + lax.rem(y, SIDE)) * 2 + core


GATHER_SEMS = 20


class PlaneGather:
    def __init__(self, buffer, first, rows, send_sem, recv_sem, sent):
        me = lax.axis_index("prow")
        self.buffer, self.sent = buffer, sent
        self.send_sem, self.recv_sem = send_sem, recv_sem
        self.core, chip = lax.rem(me, 2), me // 2
        self.cx, self.cy = chip // SIDE, lax.rem(chip, SIDE)
        self.me = me
        self.rows = [pl.ds(first, rows // 2), pl.ds(first + rows // 2, rows // 2)]
        self.events = [
            self.start,
            lambda: self.turn(0),
            lambda: self.turn(1),
            *[lambda h=h, d=d: self.land(h, d) for d in (1, 3, 2) for h in (0, 1)],
            self.end,
        ]
        self.at_event = 0

    def one(self, h, d):
        if h == 0:
            x, y = lax.rem(self.cx + d, SIDE), self.cy
        else:
            x, y = self.cx, lax.rem(self.cy + d, SIDE)
        return self.buffer.at[self.core * SIDE + x, y, self.rows[h]]

    def line(self, h, d, core):
        if h == 0:
            y = lax.rem(self.cy + d, SIDE)
            return self.buffer.at[pl.ds(core * SIDE, SIDE), y, self.rows[h]]
        x = lax.rem(self.cx + d, SIDE)
        return self.buffer.at[core * SIDE + x, :, self.rows[h]]

    def device(self, h, d):
        x, y = (self.cx + d, self.cy) if h == 0 else (self.cx, self.cy + d)
        return place(x, y, self.core)

    def copy(self, index, part, target):
        return remote(
            part, part, self.send_sem.at[index], self.recv_sem.at[index], {"prow": target}
        )

    def send(self, index, part, target):
        copy = self.copy(index, part, target)
        copy.start()
        self.sent.append(copy)

    def arrive(self, index, part):
        self.copy(index, part, self.me).wait_recv()

    def across(self, h, d):
        other = place(self.cx, self.cy, 1 - self.core)
        self.send(12 + h * 4 + d, self.line(h, d, self.core), other)

    def start(self):
        for d in (1, 3, 2):
            for h in (0, 1):
                self.send(h * 3 + d - 1, self.one(h, 0), self.device(h, d))

    def turn(self, h):
        for d in (1, 3, 2):
            self.arrive(h * 3 + d - 1, self.one(h, SIDE - d))
        for d in (1, 3, 2):
            self.send(6 + h * 3 + d - 1, self.line(h, 0, self.core), self.device(1 - h, d))
        self.across(h, 0)

    def land(self, h, d):
        self.arrive(6 + h * 3 + d - 1, self.line(h, SIDE - d, self.core))
        self.across(h, SIDE - d)

    def end(self):
        for h in (0, 1):
            for d in (0, 3, 1, 2):
                self.arrive(12 + h * 4 + d, self.line(h, d, 1 - self.core))

    def step(self):
        if self.at_event < len(self.events):
            self.events[self.at_event]()
            self.at_event += 1

    def drain(self):
        while self.at_event < len(self.events):
            self.step()


class RingSpread:
    def __init__(self, view, total, above, own, lag, skew, send_sem, recv_sem):
        self.view, self.total, self.skew = view, total, skew
        self.send_sem, self.recv_sem = send_sem, recv_sem
        z = lax.axis_index("pcol")
        inner = z < STEPS
        self.own = jnp.where(inner, own, 0)
        self.seq = [
            (jnp.where(inner, above, 0), jnp.where(inner, total, self.meet(z))),
            (jnp.where(inner, 0, self.meet(z)), jnp.where(inner, above + own, total)),
        ]
        before = lax.rem(z + RING - 1, RING)
        self.outs = [
            (
                self.seq[0][0],
                jnp.where(
                    z == RING - 1,
                    self.seq[0][0],
                    jnp.where(z < STEPS - 1, total, self.meet(z + 1)),
                ),
            ),
            (
                jnp.where(
                    z == STEPS, self.seq[1][1], jnp.where(before >= STEPS, self.meet(before), 0)
                ),
                self.seq[1][1],
            ),
        ]
        self.to = [{"pcol": lax.rem(z + 1, RING)}, {"pcol": before}]
        self.lag = [
            jnp.where(inner, 0, (z - 3) * lag),
            jnp.where(inner, 0, (RING - z) * lag),
        ]
        self.done = 0
        self.steps = total
        for c in range(STEPS, RING):
            met = min(max((2 * total + (19 - 2 * c) * skew) // 4, 0), total)
            self.steps = max(
                self.steps, (c - 3) * lag + met, (RING - c) * lag + total - met
            )

    def meet(self, z):
        return jnp.clip((2 * self.total + (19 - 2 * z) * self.skew) // 4, 0, self.total)

    def copy(self, way, g):
        return remote(
            self.view(g),
            self.view(g),
            self.send_sem.at[way, g],
            self.recv_sem.at[way, g],
            self.to[way],
        )

    def pass_on(self, way, g):
        low, high = self.outs[way]

        @pl.when((g >= low) & (g < high))
        def _():
            earlier = g - WINDOW if way == 0 else g + WINDOW

            @pl.when((earlier >= low) & (earlier < high))
            def _():
                self.copy(way, earlier).wait_send()

            self.copy(way, g).start()

    def run(self, count):
        begin, end = self.done, min(self.done + count, self.steps)
        if end <= begin:
            return
        self.done = end

        @pl.loop(begin, end)
        def _(t):
            for way in (0, 1):
                low, high = self.seq[way]
                i = t - self.lag[way]

                @pl.when((i >= 0) & (i < high - low))
                def _():
                    g = low + i if way == 0 else high - 1 - i

                    @pl.when(i >= self.own)
                    def _():
                        self.copy(way, g).wait_recv()

                    self.pass_on(way, g)

    def finish(self):
        for way in (0, 1):
            low, high = self.outs[way]

            @pl.loop(0, WINDOW)
            def _(i):
                g = high - 1 - i if way == 0 else low + i

                @pl.when((g >= low) & (g < high))
                def _():
                    self.copy(way, g).wait_send()


def weave(*streams):
    order = sorted(
        ((i + 0.5) / count, n) for n, (_, count) in enumerate(streams) for i in range(count)
    )
    for _, n in order:
        streams[n][0]()


def signal(target):
    pl.semaphore_signal(
        pltpu.get_barrier_semaphore(),
        inc=1,
        device_id=target,
        device_id_type=pl.DeviceIdType.MESH,
    )


def split(value):
    high = value.astype(BF16)
    return high, (value - high.astype(F32)).astype(BF16)


def dot(left, right):
    return jnp.dot(left, right, preferred_element_type=F32)


def choose(onehot, value):
    high, rest = split(value)
    middle = (value - high.astype(F32)) - rest.astype(F32)
    return (dot(onehot, high) + dot(onehot, rest)) + dot(onehot, middle.astype(BF16))


def main_kernel(
    source_ref, slot_ref, a_ref, local_ref, lanes_ref, inv_ref,
    out_ref,
    cand_ref, tops_ref, panels_ref, corner_ref, moved_ref, moved_panels_ref, pack_ref, dealt_ref,
    work, high_ref, low_ref, keep,
    slot_send, slot_recv, top_send, top_recv, corner_send, corner_recv,
    share_send, share_recv, deal_send, deal_recv,
    raw_send, raw_recv, first_send, first_recv, late_send, late_recv,
):
    me, z = lax.axis_index("prow"), lax.axis_index("pcol")
    core, chip = lax.rem(me, 2), me // 2
    cx, cy = chip // SIDE, lax.rem(chip, SIDE)
    block = me // 8
    dealing = z < STEPS

    signal({"pcol": lax.rem(z + 1, RING)})
    signal({"pcol": lax.rem(z + RING - 1, RING)})

    @pl.when(dealing)
    def _():
        @pl.loop(1, PROWS)
        def _(i):
            signal({"prow": lax.rem(me + i, PROWS)})

    @pl.when(z >= STEPS)
    def _():
        signal({"prow": place(cx + 1, cy, core)})
        signal({"prow": place(cx + 3, cy, core)})
        signal({"prow": place(cx + 2, cy, core)})
        signal({"prow": place(cx, cy + 2, core)})
        signal({"prow": place(cx, cy + 1, core)})
        signal({"prow": place(cx, cy + 3, core)})
        signal({"prow": place(cx, cy, 1 - core)})
        for p in range(STEPS):

            @pl.when(me != p)
            def _():
                signal({"prow": p})

    side = core * SIDE + cx

    @pl.loop(0, SLOTS, unroll=8)
    def _(s):
        cand_ref[side, cy, pl.ds(s, 1), :] = a_ref[pl.ds(slot_ref[0, s], 1), :]

    for p in range(STEPS):

        @pl.when(me == p)
        def _():
            tops_ref[side, cy, 8 * p : 8 * p + 8, :] = a_ref[8 * p : 8 * p + 8, :]

        @pl.when(z == p)
        def _():
            panels_ref[p] = a_ref[:, 0:NB]

    @pl.when(dealing)
    def _():
        row_at = lax.broadcasted_iota(jnp.int32, (NB, WIDE), 1).astype(F32)

        @pl.loop(0, STEPS)
        def _(k):
            rows = pl.ds(pl.multiple_of(k * NB, NB), NB)
            onehot = jnp.where(local_ref[rows, :] == row_at, 1.0, 0.0).astype(BF16)
            pack_ref[rows, :] = choose(onehot, a_ref[:, 0:NB])

        dealt_ref[pl.ds(pl.multiple_of(me * DEAL, DEAL), DEAL), :] = pack_ref[
            pl.ds(pl.multiple_of(me * DEAL, DEAL), DEAL), :
        ]

    met = jnp.where(me < STEPS, 9 + PROWS - 1, 9)
    pl.semaphore_wait(pltpu.get_barrier_semaphore(), jnp.where(dealing, PROWS + 1, met))

    def share(p, target):
        rows = pl.ds(pl.multiple_of(8 * p, 8), 8)
        far = target // 2
        return remote(
            a_ref.at[pl.ds(pl.multiple_of(target * 8, 8), 8), :],
            tops_ref.at[lax.rem(target, 2) * SIDE + far // SIDE, lax.rem(far, SIDE), rows],
            share_send.at[target],
            share_recv.at[p],
            {"prow": target},
        )

    def deal(source, target):
        return remote(
            pack_ref.at[pl.ds(pl.multiple_of(target * DEAL, DEAL), DEAL), :],
            dealt_ref.at[pl.ds(pl.multiple_of(source * DEAL, DEAL), DEAL), :],
            deal_send.at[target],
            deal_recv.at[source],
            {"prow": target},
        )

    @pl.when(me < STEPS)
    def _():
        @pl.loop(1, PROWS)
        def _(i):
            share(me, lax.rem(me + i, PROWS)).start()

    @pl.when(dealing)
    def _():
        @pl.loop(1, PROWS)
        def _(i):
            target = lax.rem(me + i, PROWS)

            @pl.when(target // 8 != z)
            def _():
                deal(me, target).start()

    per = WIDE // CHUNK

    def raw_view(g):
        return panels_ref.at[
            3 - g // per, pl.ds(pl.multiple_of(lax.rem(g, per) * CHUNK, CHUNK), CHUNK), :
        ]

    def first_view(g):
        return corner_ref.at[side, cy, pl.ds(pl.multiple_of(g * 32, 32), 32)]

    late = SLOTS // LATE

    def late_view(g):
        return moved_panels_ref.at[
            3 - g // late, pl.ds(pl.multiple_of(lax.rem(g, late) * LATE, LATE), LATE), :
        ]

    raw = RingSpread(raw_view, STEPS * per, (3 - z) * per, per, 4, 8, raw_send, raw_recv)
    above = 3 - z - jnp.where(block > z, 1, 0)
    mine = jnp.where(block == z, 0, 1)
    first = RingSpread(first_view, 3, above, mine, 4, 8, first_send, first_recv)
    moved = RingSpread(
        late_view, STEPS * late, (3 - z) * late, late, 4, 8, late_send, late_recv
    )
    sent = []
    slots = PlaneGather(cand_ref, 0, SLOTS, slot_send, slot_recv, sent)
    tops = PlaneGather(tops_ref, 0, TOPS, top_send, top_recv, sent)
    corner = PlaneGather(corner_ref, 0, 96, corner_send, corner_recv, sent)

    def row_of(index):
        return cand_ref[index >> 9, (index >> 7) & 3, pl.ds(index & 127, 1), :]

    chosen = [0]

    def choose_rows():
        n = chosen[0]
        chosen[0] += 1

        @pl.loop(0, 32, unroll=8)
        def _(j):
            work[pl.ds(n * 32 + j, 1), PAN:] = row_of(source_ref[n // 8, n % 8 * 32 + j])

    def advance(*rings):
        return [(lambda ring=ring: ring.run(1), count) for ring, count in rings]

    slots.step()
    raw.run(PLAN[0])
    for p in range(STEPS):

        @pl.when(me != p)
        def _():
            share(p, me).wait_recv()

    tops.step()
    raw.run(PLAN[1])
    tops.step()
    tops.step()
    raw.run(PLAN[2])

    @pl.when(dealing & (block != z))
    def _():
        @pl.loop(1, PROWS)
        def _(i):
            deal(lax.rem(me + i, PROWS), me).wait_recv()

        total = dealt_ref[0:DEAL, :]
        for p in range(1, PROWS):
            total += dealt_ref[p * DEAL : (p + 1) * DEAL, :]
        corner_ref[side, cy, pl.ds(pl.multiple_of(above * 32, 32), 32), :] = total

    weave(*advance((first, PLAN[3]), (raw, PLAN[3])), (tops.step, 7))

    @pl.loop(0, SLOTS, unroll=8)
    def _(s):
        index = slot_ref[1, s]
        moved_ref[pl.ds(s, 1), :] = tops_ref[
            index >> 9, (index >> 7) & 3, pl.ds(index & 127, 1), :
        ]

    for p in range(STEPS):

        @pl.when(z == p)
        def _():
            moved_panels_ref[p] = moved_ref[:, 0:NB]

    slots.step()
    slots.step()
    left = first.steps - PLAN[3]
    weave(*advance((first, left), (raw, left), (moved, left)))
    corner.step()
    weave(*advance((moved, PLAN[4]), (raw, PLAN[4])))
    corner.step()
    corner.step()
    weave(*advance((moved, PLAN[5]), (raw, PLAN[5])), (slots.step, 7))
    moved.run(moved.steps)
    cand_ref[:, :, SLOTS:, :] = tops_ref[...]
    weave(*advance((raw, PLAN[6])), (corner.step, 7), (choose_rows, 32))


    slot_at = lanes_ref[0:1, :]
    row_at = lax.broadcasted_iota(jnp.int32, (WIDE, 128), 0).astype(F32)
    step_at = lax.broadcasted_iota(jnp.int32, (WIDE, 128), 1) // CAP
    match = jnp.where(row_at == slot_at, 1.0, 0.0)
    last = jnp.max(jnp.where(match > 0.0, step_at.astype(F32), -1.0), axis=1, keepdims=True)
    hit = last >= 0.0
    onehot = jnp.where((step_at.astype(F32) == last) & (match > 0.0), 1.0, 0.0)
    onehot = onehot.astype(BF16)[:, 0:SLOTS]
    for c in range(0, WIDE, NB):
        work[PAN:, PAN + c : PAN + c + NB] = jnp.where(
            hit, choose(onehot, moved_ref[:, c : c + NB]), a_ref[:, c : c + NB]
        )

    for k in range(STEPS):
        for q in range(STEPS):
            if q != k:
                g = 3 - q - (1 if k > q else 0)
                for i in range(8):
                    far = k * 4 + i // 2
                    work[k * NB + i * 32 : k * NB + i * 32 + 32, q * NB : (q + 1) * NB] = (
                        corner_ref[
                            i % 2 * SIDE + far // SIDE, far % SIDE, g * 32 : g * 32 + 32, :
                        ]
                    )
    row_i = lax.broadcasted_iota(jnp.int32, (NB, NB), 0)
    col_i = lax.broadcasted_iota(jnp.int32, (NB, NB), 1)
    total = PAN + WIDE

    def eliminate(k, rows):
        top, begin = k * NB, (k + 1) * NB
        upper = jnp.where(row_i <= col_i, inv_ref[k].astype(F32), 0.0).astype(BF16)
        high, low = split(work[rows, top : top + NB])
        factor = dot(high, upper) + dot(low, upper)
        work[rows, top : top + NB] = factor
        high, low = split(factor)
        for c in range(begin, total, NB):
            work[rows, c : c + NB] -= (
                dot(high, high_ref[top : top + NB, c : c + NB])
                + dot(high, low_ref[top : top + NB, c : c + NB])
                + dot(low, high_ref[top : top + NB, c : c + NB])
            )

    for k in range(STEPS):
        top, begin = k * NB, (k + 1) * NB
        lower = jnp.where(
            row_i > col_i, inv_ref[k].astype(F32), jnp.where(row_i == col_i, 1.0, 0.0)
        ).astype(BF16)

        @pl.when(me == k)
        def _():
            keep[...] = work[top : top + NB, PAN : PAN + NB]

        for c in range(begin, total, NB):
            high, low = split(work[top : top + NB, c : c + NB])
            solved = dot(lower, high) + dot(lower, low)
            work[top : top + NB, c : c + NB] = solved
            high, low = split(solved)
            high_ref[top : top + NB, c : c + NB] = high
            low_ref[top : top + NB, c : c + NB] = low
        raw.run(2)
        if begin < PAN:

            @pl.loop(k + 1, STEPS)
            def _(r):
                eliminate(k, pl.ds(pl.multiple_of(r * NB, NB), NB))

            raw.run(2)

    raw.run(raw.steps)
    for q in range(STEPS):
        work[PAN:, q * NB : (q + 1) * NB] = jnp.where(
            hit, choose(onehot, moved_panels_ref[q]), panels_ref[q]
        )

    @pl.loop(STEPS, total // NB)
    def _(r):
        for k in range(STEPS):
            eliminate(k, pl.ds(pl.multiple_of(r * NB, NB), NB))

    out_ref[...] = work[PAN:, PAN:]
    for q in range(STEPS):

        @pl.when(z == q)
        def _():
            out_ref[:, 0:NB] = work[PAN:, q * NB : (q + 1) * NB]

    for p in range(STEPS):

        @pl.when(me == p)
        def _():
            out_ref[0:NB, :] = work[p * NB : (p + 1) * NB, PAN:]
            for q in range(p):

                @pl.when(z == q)
                def _():
                    out_ref[0:NB, 0:NB] = work[p * NB : (p + 1) * NB, q * NB : (q + 1) * NB]

            @pl.when(z == p)
            def _():
                out_ref[0:NB, 0:NB] = keep[...]

    for copy in sent:
        copy.wait_send()
    for ring in (raw, first, moved):
        ring.finish()

    @pl.when(me < STEPS)
    def _():
        @pl.loop(1, PROWS)
        def _(i):
            share(me, lax.rem(me + i, PROWS)).wait_send()

    @pl.when(dealing)
    def _():
        @pl.loop(1, PROWS)
        def _(i):
            target = lax.rem(me + i, PROWS)

            @pl.when(target // 8 != z)
            def _():
                deal(me, target).wait_send()


PLAN = (12, 6, 10, 10, 5, 8, 8)
VMEM = pl.BlockSpec(memory_space=pltpu.VMEM)
SMEM = pl.BlockSpec(memory_space=pltpu.SMEM)


def shape(*dims, dtype=F32):
    return jax.ShapeDtypeStruct(dims, dtype)


def prepare(coord, pivots):
    return pl.pallas_call(
        prep_kernel,
        out_shape=[
            shape(8, NB, dtype=jnp.int32),
            shape(8, 128, dtype=jnp.int32),
            shape(PAN, 1),
            shape(8, 128),
        ],
        in_specs=[SMEM, VMEM],
        out_specs=[VMEM] * 4,
        compiler_params=pltpu.CompilerParams(vmem_limit_bytes=16 * MIB),
    )(coord, pivots)


def factor(source, slot, matrix, local, lanes, inverses):
    dma = pltpu.SemaphoreType.DMA
    raw, late = STEPS * WIDE // CHUNK, STEPS * SLOTS // LATE
    return pl.pallas_call(
        main_kernel,
        out_shape=shape(WIDE, WIDE),
        in_specs=[SMEM] * 2 + [VMEM] * 4,
        out_specs=VMEM,
        scratch_shapes=[
            pltpu.VMEM((2 * SIDE, SIDE, PIECE, WIDE), F32),
            pltpu.VMEM((2 * SIDE, SIDE, TOPS, WIDE), F32),
            pltpu.VMEM((STEPS, WIDE, NB), F32),
            pltpu.VMEM((2 * SIDE, SIDE, 96, NB), F32),
            pltpu.VMEM((SLOTS, WIDE), F32),
            pltpu.VMEM((STEPS, SLOTS, NB), F32),
            pltpu.VMEM((PAN, NB), F32),
            pltpu.VMEM((PAN, NB), F32),
            pltpu.VMEM((PAN + WIDE, PAN + WIDE), F32),
            pltpu.VMEM((PAN, PAN + WIDE), BF16),
            pltpu.VMEM((PAN, PAN + WIDE), BF16),
            pltpu.VMEM((NB, NB), F32),
            *[dma((GATHER_SEMS,))] * 6,
            dma((PROWS,)), dma((STEPS,)), dma((PROWS,)), dma((PROWS,)),
            dma((2, raw)), dma((2, raw)), dma((2, 3)), dma((2, 3)),
            dma((2, late)), dma((2, late)),
        ],
        compiler_params=pltpu.CompilerParams(
            vmem_limit_bytes=52 * MIB, collective_id=0, has_side_effects=True
        ),
    )(source, slot, matrix, local, lanes, inverses)


def per_device(matrix, pivots, block_inverses):
    coord = jnp.stack([lax.axis_index("prow"), lax.axis_index("pcol")]).astype(jnp.int32)
    source, slot, local, lanes = prepare(coord, pivots)
    return factor(source, slot, matrix, local, lanes, block_inverses)


def solution(mesh):
    placed = (P("prow", "pcol"), P(), P())
    return jax.shard_map(
        per_device, mesh=mesh, in_specs=placed, out_specs=P("prow", "pcol"), check_vma=False
    )
```

```python
import jax
import jax.numpy as jnp
from jax import lax
from jax.experimental import pallas as pl
from jax.experimental.pallas import tpu as pltpu
from jax.sharding import PartitionSpec as P

NB = 256
STEPS = 4
CAP = 16
SLOTS = STEPS * CAP
TOPS = 32
PIECE = SLOTS + TOPS
DEAL = 32
WINDOW = 4
SIDE = 4
PROWS = 32
RING = 16
WIDE = 512
PAN = STEPS * NB
CHUNK = 32
LATE = 32
F32 = jnp.float32
BF16 = jnp.bfloat16
MIB = 1024 * 1024


def prep_kernel(coord, piv_ref, source_ref, slot_ref, local_ref, lanes_ref):
    me = coord[0].astype(F32)
    sub = lax.broadcasted_iota(jnp.int32, (NB, NB), 0)
    lane = lax.broadcasted_iota(jnp.int32, (NB, NB), 1)
    lane_row = lax.broadcasted_iota(jnp.int32, (1, NB), 1).astype(F32)
    lane_slot = lax.broadcasted_iota(jnp.int32, (NB, 128), 1).astype(F32)

    def column(row):
        return jnp.sum(jnp.where(sub == lane, row, 0.0), axis=1, keepdims=True)

    def pick(mask, value):
        return jnp.sum(jnp.where(mask, value, 0.0), axis=0, keepdims=True)

    def top_index(row):
        t = row.astype(jnp.int32)
        return piece_index((t & 255) >> 3) + SLOTS + (t >> 8) * 8 + (t & 7)

    def piece_index(p):
        return ((p & 1) * 16 + (p >> 1)) << 7

    source_ref[...] = jnp.zeros_like(source_ref)
    slot_ref[...] = jnp.zeros_like(slot_ref)
    filled = jnp.zeros((1, 128), F32)
    slot_row = jnp.zeros((1, 128), F32)
    slot_top = jnp.zeros((1, 128), F32)
    pivot_cols, moved_cols = [], []
    for k in range(STEPS):
        pivot = piv_ref[k : k + 1, :]
        owner = ((pivot >> 8) & 31).astype(F32)
        local = (((pivot >> 13) << 8) | (pivot & 255)).astype(F32)
        pivot = pivot.astype(F32)
        owner_col, local_col, pivot_col = column(owner), column(local), column(pivot)
        rank = pick((owner_col == owner) & (sub < lane), 1.0) + float(k * CAP)
        rank_col = column(rank)
        position = lane_row + float(k * NB)
        moved = position
        source = piece_index(owner.astype(jnp.int32)) + rank.astype(jnp.int32)
        mine = jnp.where(owner == me, local, -1.0)
        for earlier in range(k):
            same = pivot_cols[earlier] == position
            moved = jnp.where(pick(same, 1.0) > 0.0, pick(same, moved_cols[earlier]), moved)
            same = pivot_cols[earlier] == pivot
            hit = pick(same, 1.0) > 0.0
            top = pick(same, moved_cols[earlier])
            source = jnp.where(hit, top_index(top), source)
            block = (top.astype(jnp.int32) >> 8).astype(F32)
            mine = jnp.where(hit, jnp.where(block == me, top - block * NB, -1.0), mine)
        moved_col = column(moved)
        pivot_cols.append(pivot_col)
        moved_cols.append(moved_col)
        source_ref[k : k + 1, :] = source
        local_ref[k * NB : (k + 1) * NB, :] = column(mine)
        here = (owner_col == me) & (rank_col == lane_slot)
        filled += pick(here, 1.0)
        slot_row += pick(here, local_col)
        slot_top += pick(here, moved_col)
    slot_ref[0:1, :] = slot_row.astype(jnp.int32)
    slot_ref[1:2, :] = top_index(slot_top) - SLOTS
    lanes_ref[...] = jnp.broadcast_to(jnp.where(filled > 0.0, slot_row, -1.0), (8, 128))


def remote(src, dst, send_sem, recv_sem, target):
    return pltpu.make_async_remote_copy(
        src_ref=src,
        dst_ref=dst,
        send_sem=send_sem,
        recv_sem=recv_sem,
        device_id=target,
        device_id_type=pl.DeviceIdType.MESH,
    )


def place(x, y, core):
    return (lax.rem(x, SIDE) * SIDE + lax.rem(y, SIDE)) * 2 + core


GATHER_SEMS = 20


class PlaneGather:
    def __init__(self, buffer, first, rows, send_sem, recv_sem, sent):
        me = lax.axis_index("prow")
        self.buffer, self.sent = buffer, sent
        self.send_sem, self.recv_sem = send_sem, recv_sem
        self.core, chip = lax.rem(me, 2), me // 2
        self.cx, self.cy = chip // SIDE, lax.rem(chip, SIDE)
        self.me = me
        self.rows = [pl.ds(first, rows // 2), pl.ds(first + rows // 2, rows // 2)]
        self.events = [
            self.start,
            lambda: self.turn(0),
            lambda: self.turn(1),
            *[lambda h=h, d=d: self.land(h, d) for d in (1, 3, 2) for h in (0, 1)],
            self.end,
        ]
        self.at_event = 0

    def one(self, h, d):
        if h == 0:
            x, y = lax.rem(self.cx + d, SIDE), self.cy
        else:
            x, y = self.cx, lax.rem(self.cy + d, SIDE)
        return self.buffer.at[self.core * SIDE + x, y, self.rows[h]]

    def line(self, h, d, core):
        if h == 0:
            y = lax.rem(self.cy + d, SIDE)
            return self.buffer.at[pl.ds(core * SIDE, SIDE), y, self.rows[h]]
        x = lax.rem(self.cx + d, SIDE)
        return self.buffer.at[core * SIDE + x, :, self.rows[h]]

    def device(self, h, d):
        x, y = (self.cx + d, self.cy) if h == 0 else (self.cx, self.cy + d)
        return place(x, y, self.core)

    def copy(self, index, part, target):
        return remote(
            part, part, self.send_sem.at[index], self.recv_sem.at[index], {"prow": target}
        )

    def send(self, index, part, target):
        copy = self.copy(index, part, target)
        copy.start()
        self.sent.append(copy)

    def arrive(self, index, part):
        self.copy(index, part, self.me).wait_recv()

    def across(self, h, d):
        other = place(self.cx, self.cy, 1 - self.core)
        self.send(12 + h * 4 + d, self.line(h, d, self.core), other)

    def start(self):
        for d in (1, 3, 2):
            for h in (0, 1):
                self.send(h * 3 + d - 1, self.one(h, 0), self.device(h, d))

    def turn(self, h):
        for d in (1, 3, 2):
            self.arrive(h * 3 + d - 1, self.one(h, SIDE - d))
        for d in (1, 3, 2):
            self.send(6 + h * 3 + d - 1, self.line(h, 0, self.core), self.device(1 - h, d))
        self.across(h, 0)

    def land(self, h, d):
        self.arrive(6 + h * 3 + d - 1, self.line(h, SIDE - d, self.core))
        self.across(h, SIDE - d)

    def end(self):
        for h in (0, 1):
            for d in (0, 3, 1, 2):
                self.arrive(12 + h * 4 + d, self.line(h, d, 1 - self.core))

    def step(self):
        if self.at_event < len(self.events):
            self.events[self.at_event]()
            self.at_event += 1

    def drain(self):
        while self.at_event < len(self.events):
            self.step()


class RingSpread:
    def __init__(self, view, total, above, own, lag, skew, send_sem, recv_sem):
        self.view, self.total, self.skew = view, total, skew
        self.send_sem, self.recv_sem = send_sem, recv_sem
        z = lax.axis_index("pcol")
        inner = z < STEPS
        self.own = jnp.where(inner, own, 0)
        self.seq = [
            (jnp.where(inner, above, 0), jnp.where(inner, total, self.meet(z))),
            (jnp.where(inner, 0, self.meet(z)), jnp.where(inner, above + own, total)),
        ]
        before = lax.rem(z + RING - 1, RING)
        self.outs = [
            (
                self.seq[0][0],
                jnp.where(
                    z == RING - 1,
                    self.seq[0][0],
                    jnp.where(z < STEPS - 1, total, self.meet(z + 1)),
                ),
            ),
            (
                jnp.where(
                    z == STEPS, self.seq[1][1], jnp.where(before >= STEPS, self.meet(before), 0)
                ),
                self.seq[1][1],
            ),
        ]
        self.to = [{"pcol": lax.rem(z + 1, RING)}, {"pcol": before}]
        self.lag = [
            jnp.where(inner, 0, (z - 3) * lag),
            jnp.where(inner, 0, (RING - z) * lag),
        ]
        self.done = 0
        self.steps = total
        for c in range(STEPS, RING):
            met = min(max((2 * total + (19 - 2 * c) * skew) // 4, 0), total)
            self.steps = max(
                self.steps, (c - 3) * lag + met, (RING - c) * lag + total - met
            )

    def meet(self, z):
        return jnp.clip((2 * self.total + (19 - 2 * z) * self.skew) // 4, 0, self.total)

    def copy(self, way, g):
        return remote(
            self.view(g),
            self.view(g),
            self.send_sem.at[way, g],
            self.recv_sem.at[way, g],
            self.to[way],
        )

    def pass_on(self, way, g):
        low, high = self.outs[way]

        @pl.when((g >= low) & (g < high))
        def _():
            earlier = g - WINDOW if way == 0 else g + WINDOW

            @pl.when((earlier >= low) & (earlier < high))
            def _():
                self.copy(way, earlier).wait_send()

            self.copy(way, g).start()

    def run(self, count):
        begin, end = self.done, min(self.done + count, self.steps)
        if end <= begin:
            return
        self.done = end

        @pl.loop(begin, end)
        def _(t):
            for way in (0, 1):
                low, high = self.seq[way]
                i = t - self.lag[way]

                @pl.when((i >= 0) & (i < high - low))
                def _():
                    g = low + i if way == 0 else high - 1 - i

                    @pl.when(i >= self.own)
                    def _():
                        self.copy(way, g).wait_recv()

                    self.pass_on(way, g)

    def finish(self):
        for way in (0, 1):
            low, high = self.outs[way]

            @pl.loop(0, WINDOW)
            def _(i):
                g = high - 1 - i if way == 0 else low + i

                @pl.when((g >= low) & (g < high))
                def _():
                    self.copy(way, g).wait_send()


def weave(*streams):
    order = sorted(
        ((i + 0.5) / count, n) for n, (_, count) in enumerate(streams) for i in range(count)
    )
    for _, n in order:
        streams[n][0]()


def signal(target):
    pl.semaphore_signal(
        pltpu.get_barrier_semaphore(),
        inc=1,
        device_id=target,
        device_id_type=pl.DeviceIdType.MESH,
    )


def split(value):
    high = value.astype(BF16)
    return high, (value - high.astype(F32)).astype(BF16)


def dot(left, right):
    return jnp.dot(left, right, preferred_element_type=F32)


def choose(onehot, value):
    high, rest = split(value)
    middle = (value - high.astype(F32)) - rest.astype(F32)
    return (dot(onehot, high) + dot(onehot, rest)) + dot(onehot, middle.astype(BF16))


def main_kernel(
    source_ref, slot_ref, a_ref, local_ref, lanes_ref, inv_ref,
    out_ref,
    cand_ref, tops_ref, panels_ref, corner_ref, moved_ref, moved_panels_ref, pack_ref, dealt_ref,
    work, parts_ref, keep,
    slot_send, slot_recv, top_send, top_recv, corner_send, corner_recv,
    share_send, share_recv, deal_send, deal_recv,
    raw_send, raw_recv, first_send, first_recv, late_send, late_recv,
):
    me, z = lax.axis_index("prow"), lax.axis_index("pcol")
    core, chip = lax.rem(me, 2), me // 2
    cx, cy = chip // SIDE, lax.rem(chip, SIDE)
    block = me // 8
    dealing = z < STEPS

    signal({"pcol": lax.rem(z + 1, RING)})
    signal({"pcol": lax.rem(z + RING - 1, RING)})

    @pl.when(dealing)
    def _():
        @pl.loop(1, PROWS)
        def _(i):
            signal({"prow": lax.rem(me + i, PROWS)})

    @pl.when(z >= STEPS)
    def _():
        signal({"prow": place(cx + 1, cy, core)})
        signal({"prow": place(cx + 3, cy, core)})
        signal({"prow": place(cx + 2, cy, core)})
        signal({"prow": place(cx, cy + 2, core)})
        signal({"prow": place(cx, cy + 1, core)})
        signal({"prow": place(cx, cy + 3, core)})
        signal({"prow": place(cx, cy, 1 - core)})
        for p in range(STEPS):

            @pl.when(me != p)
            def _():
                signal({"prow": p})

    side = core * SIDE + cx

    @pl.loop(0, SLOTS, unroll=8)
    def _(s):
        cand_ref[side, cy, pl.ds(s, 1), :] = a_ref[pl.ds(slot_ref[0, s], 1), :]

    for p in range(STEPS):

        @pl.when(me == p)
        def _():
            tops_ref[side, cy, 8 * p : 8 * p + 8, :] = a_ref[8 * p : 8 * p + 8, :]

        @pl.when(z == p)
        def _():
            panels_ref[p] = a_ref[:, 0:NB]

    @pl.when(dealing)
    def _():
        row_at = lax.broadcasted_iota(jnp.int32, (NB, WIDE), 1).astype(F32)

        @pl.loop(0, STEPS)
        def _(k):
            rows = pl.ds(pl.multiple_of(k * NB, NB), NB)
            onehot = jnp.where(local_ref[rows, :] == row_at, 1.0, 0.0).astype(BF16)
            pack_ref[rows, :] = choose(onehot, a_ref[:, 0:NB])

        dealt_ref[pl.ds(pl.multiple_of(me * DEAL, DEAL), DEAL), :] = pack_ref[
            pl.ds(pl.multiple_of(me * DEAL, DEAL), DEAL), :
        ]

    met = jnp.where(me < STEPS, 9 + PROWS - 1, 9)
    pl.semaphore_wait(pltpu.get_barrier_semaphore(), jnp.where(dealing, PROWS + 1, met))

    def share(p, target):
        rows = pl.ds(pl.multiple_of(8 * p, 8), 8)
        far = target // 2
        return remote(
            a_ref.at[pl.ds(pl.multiple_of(target * 8, 8), 8), :],
            tops_ref.at[lax.rem(target, 2) * SIDE + far // SIDE, lax.rem(far, SIDE), rows],
            share_send.at[target],
            share_recv.at[p],
            {"prow": target},
        )

    def deal(source, target):
        return remote(
            pack_ref.at[pl.ds(pl.multiple_of(target * DEAL, DEAL), DEAL), :],
            dealt_ref.at[pl.ds(pl.multiple_of(source * DEAL, DEAL), DEAL), :],
            deal_send.at[target],
            deal_recv.at[source],
            {"prow": target},
        )

    @pl.when(me < STEPS)
    def _():
        @pl.loop(1, PROWS)
        def _(i):
            share(me, lax.rem(me + i, PROWS)).start()

    @pl.when(dealing)
    def _():
        @pl.loop(1, PROWS)
        def _(i):
            target = lax.rem(me + i, PROWS)

            @pl.when(target // 8 != z)
            def _():
                deal(me, target).start()

    per = WIDE // CHUNK

    def raw_view(g):
        return panels_ref.at[
            3 - g // per, pl.ds(pl.multiple_of(lax.rem(g, per) * CHUNK, CHUNK), CHUNK), :
        ]

    def first_view(g):
        return corner_ref.at[side, cy, pl.ds(pl.multiple_of(g * 32, 32), 32)]

    late = SLOTS // LATE

    def late_view(g):
        return moved_panels_ref.at[
            3 - g // late, pl.ds(pl.multiple_of(lax.rem(g, late) * LATE, LATE), LATE), :
        ]

    raw = RingSpread(raw_view, STEPS * per, (3 - z) * per, per, 4, 8, raw_send, raw_recv)
    above = 3 - z - jnp.where(block > z, 1, 0)
    mine = jnp.where(block == z, 0, 1)
    first = RingSpread(first_view, 3, above, mine, 3, 8, first_send, first_recv)
    moved = RingSpread(
        late_view, STEPS * late, (3 - z) * late, late, 3, 8, late_send, late_recv
    )
    sent = []
    slots = PlaneGather(cand_ref, 0, SLOTS, slot_send, slot_recv, sent)
    tops = PlaneGather(tops_ref, 0, TOPS, top_send, top_recv, sent)
    corner = PlaneGather(corner_ref, 0, 96, corner_send, corner_recv, sent)

    def row_of(index):
        return cand_ref[index >> 9, (index >> 7) & 3, pl.ds(index & 127, 1), :]

    chosen = [0]

    def choose_rows():
        n = chosen[0]
        chosen[0] += 1

        @pl.loop(0, 32, unroll=8)
        def _(j):
            work[pl.ds(n * 32 + j, 1), PAN:] = row_of(source_ref[n // 8, n % 8 * 32 + j])

    def advance(*rings):
        return [(lambda ring=ring: ring.run(1), count) for ring, count in rings]

    slots.step()
    raw.run(PLAN[0])
    for p in range(STEPS):

        @pl.when(me != p)
        def _():
            share(p, me).wait_recv()

    tops.step()
    raw.run(PLAN[1])
    tops.step()
    tops.step()
    raw.run(PLAN[2])

    @pl.when(dealing & (block != z))
    def _():
        @pl.loop(1, PROWS)
        def _(i):
            deal(lax.rem(me + i, PROWS), me).wait_recv()

        total = dealt_ref[0:DEAL, :]
        for p in range(1, PROWS):
            total += dealt_ref[p * DEAL : (p + 1) * DEAL, :]
        corner_ref[side, cy, pl.ds(pl.multiple_of(above * 32, 32), 32), :] = total

    weave(*advance((first, PLAN[3]), (raw, PLAN[3])), (tops.step, 7))

    @pl.loop(0, SLOTS, unroll=8)
    def _(s):
        index = slot_ref[1, s]
        moved_ref[pl.ds(s, 1), :] = tops_ref[
            index >> 9, (index >> 7) & 3, pl.ds(index & 127, 1), :
        ]

    for p in range(STEPS):

        @pl.when(z == p)
        def _():
            moved_panels_ref[p] = moved_ref[:, 0:NB]

    slots.step()
    slots.step()
    left = first.steps - PLAN[3]
    weave(*advance((first, left), (raw, left), (moved, left)))
    corner.step()
    weave(*advance((moved, PLAN[4]), (raw, PLAN[4])))
    corner.step()
    corner.step()
    weave(*advance((moved, PLAN[5]), (raw, PLAN[5])), (slots.step, 7))
    moved.run(moved.steps)
    cand_ref[:, :, SLOTS:, :] = tops_ref[...]
    weave(*advance((raw, PLAN[6])), (corner.step, 7), (choose_rows, 32))


    slot_at = lanes_ref[0:1, :]
    row_at = lax.broadcasted_iota(jnp.int32, (WIDE, 128), 0).astype(F32)
    step_at = lax.broadcasted_iota(jnp.int32, (WIDE, 128), 1) // CAP
    match = jnp.where(row_at == slot_at, 1.0, 0.0)
    last = jnp.max(jnp.where(match > 0.0, step_at.astype(F32), -1.0), axis=1, keepdims=True)
    hit = last >= 0.0
    onehot = jnp.where((step_at.astype(F32) == last) & (match > 0.0), 1.0, 0.0)
    onehot = onehot.astype(BF16)[:, 0:SLOTS]
    for c in range(0, WIDE, NB):
        work[PAN:, PAN + c : PAN + c + NB] = jnp.where(
            hit, choose(onehot, moved_ref[:, c : c + NB]), a_ref[:, c : c + NB]
        )

    for k in range(STEPS):
        for q in range(STEPS):
            if q != k:
                g = 3 - q - (1 if k > q else 0)
                for i in range(8):
                    far = k * 4 + i // 2
                    work[k * NB + i * 32 : k * NB + i * 32 + 32, q * NB : (q + 1) * NB] = (
                        corner_ref[
                            i % 2 * SIDE + far // SIDE, far % SIDE, g * 32 : g * 32 + 32, :
                        ]
                    )
    row_i = lax.broadcasted_iota(jnp.int32, (NB, NB), 0)
    col_i = lax.broadcasted_iota(jnp.int32, (NB, NB), 1)
    total = PAN + WIDE

    def eliminate(k, rows):
        top, begin = k * NB, (k + 1) * NB
        upper = jnp.where(row_i <= col_i, inv_ref[k].astype(F32), 0.0).astype(BF16)
        high, low = split(work[rows, top : top + NB])
        factor = dot(high, upper) + dot(low, upper)
        work[rows, top : top + NB] = factor
        high, low = split(factor)
        left = jnp.concatenate([high, high, low], axis=1)
        for c in range(begin, total, NB):
            work[rows, c : c + NB] -= dot(left, parts_ref[3 * top : 3 * begin, c : c + NB])

    for k in range(STEPS):
        top, begin = k * NB, (k + 1) * NB
        lower = jnp.where(
            row_i > col_i, inv_ref[k].astype(F32), jnp.where(row_i == col_i, 1.0, 0.0)
        ).astype(BF16)

        @pl.when(me == k)
        def _():
            keep[...] = work[top : top + NB, PAN : PAN + NB]

        for c in range(begin, total, NB):
            high, low = split(work[top : top + NB, c : c + NB])
            solved = dot(lower, high) + dot(lower, low)
            work[top : top + NB, c : c + NB] = solved
            high, low = split(solved)
            for n, part in enumerate((high, low, high)):
                parts_ref[3 * top + n * NB : 3 * top + (n + 1) * NB, c : c + NB] = part
        raw.run(2)
        if begin < PAN:

            @pl.loop(k + 1, STEPS)
            def _(r):
                eliminate(k, pl.ds(pl.multiple_of(r * NB, NB), NB))

            raw.run(2)

    raw.run(raw.steps)
    for q in range(STEPS):
        work[PAN:, q * NB : (q + 1) * NB] = jnp.where(
            hit, choose(onehot, moved_panels_ref[q]), panels_ref[q]
        )

    @pl.loop(STEPS, total // NB)
    def _(r):
        for k in range(STEPS):
            eliminate(k, pl.ds(pl.multiple_of(r * NB, NB), NB))

    out_ref[...] = work[PAN:, PAN:]
    for q in range(STEPS):

        @pl.when(z == q)
        def _():
            out_ref[:, 0:NB] = work[PAN:, q * NB : (q + 1) * NB]

    for p in range(STEPS):

        @pl.when(me == p)
        def _():
            out_ref[0:NB, :] = work[p * NB : (p + 1) * NB, PAN:]
            for q in range(p):

                @pl.when(z == q)
                def _():
                    out_ref[0:NB, 0:NB] = work[p * NB : (p + 1) * NB, q * NB : (q + 1) * NB]

            @pl.when(z == p)
            def _():
                out_ref[0:NB, 0:NB] = keep[...]

    for copy in sent:
        copy.wait_send()
    for ring in (raw, first, moved):
        ring.finish()

    @pl.when(me < STEPS)
    def _():
        @pl.loop(1, PROWS)
        def _(i):
            share(me, lax.rem(me + i, PROWS)).wait_send()

    @pl.when(dealing)
    def _():
        @pl.loop(1, PROWS)
        def _(i):
            target = lax.rem(me + i, PROWS)

            @pl.when(target // 8 != z)
            def _():
                deal(me, target).wait_send()


PLAN = (18, 12, 10, 4, 4, 6, 6)
VMEM = pl.BlockSpec(memory_space=pltpu.VMEM)
SMEM = pl.BlockSpec(memory_space=pltpu.SMEM)


def shape(*dims, dtype=F32):
    return jax.ShapeDtypeStruct(dims, dtype)


def prepare(coord, pivots):
    return pl.pallas_call(
        prep_kernel,
        out_shape=[
            shape(8, NB, dtype=jnp.int32),
            shape(8, 128, dtype=jnp.int32),
            shape(PAN, 1),
            shape(8, 128),
        ],
        in_specs=[SMEM, VMEM],
        out_specs=[VMEM] * 4,
        compiler_params=pltpu.CompilerParams(vmem_limit_bytes=16 * MIB),
    )(coord, pivots)


def factor(source, slot, matrix, local, lanes, inverses):
    dma = pltpu.SemaphoreType.DMA
    raw, late = STEPS * WIDE // CHUNK, STEPS * SLOTS // LATE
    return pl.pallas_call(
        main_kernel,
        out_shape=shape(WIDE, WIDE),
        in_specs=[SMEM] * 2 + [VMEM] * 4,
        out_specs=VMEM,
        scratch_shapes=[
            pltpu.VMEM((2 * SIDE, SIDE, PIECE, WIDE), F32),
            pltpu.VMEM((2 * SIDE, SIDE, TOPS, WIDE), F32),
            pltpu.VMEM((STEPS, WIDE, NB), F32),
            pltpu.VMEM((2 * SIDE, SIDE, 96, NB), F32),
            pltpu.VMEM((SLOTS, WIDE), F32),
            pltpu.VMEM((STEPS, SLOTS, NB), F32),
            pltpu.VMEM((PAN, NB), F32),
            pltpu.VMEM((PAN, NB), F32),
            pltpu.VMEM((PAN + WIDE, PAN + WIDE), F32),
            pltpu.VMEM((3 * PAN, PAN + WIDE), BF16),
            pltpu.VMEM((NB, NB), F32),
            *[dma((GATHER_SEMS,))] * 6,
            dma((PROWS,)), dma((STEPS,)), dma((PROWS,)), dma((PROWS,)),
            dma((2, raw)), dma((2, raw)), dma((2, 3)), dma((2, 3)),
            dma((2, late)), dma((2, late)),
        ],
        compiler_params=pltpu.CompilerParams(
            vmem_limit_bytes=52 * MIB, collective_id=0, has_side_effects=True
        ),
    )(source, slot, matrix, local, lanes, inverses)


def per_device(matrix, pivots, block_inverses):
    coord = jnp.stack([lax.axis_index("prow"), lax.axis_index("pcol")]).astype(jnp.int32)
    source, slot, local, lanes = prepare(coord, pivots)
    return factor(source, slot, matrix, local, lanes, block_inverses)


def solution(mesh):
    placed = (P("prow", "pcol"), P(), P())
    return jax.shard_map(
        per_device, mesh=mesh, in_specs=placed, out_specs=P("prow", "pcol"), check_vma=False
    )
```
